1024 devices in a mesh: row: 16 (over z_hi, y), col: 64 (over z_lo, x, core).
Axes of the slice: x: 4, y: 4, z: 32 (z_hi: 4, z_lo: 8; z = z_hi * 8 + z_lo), core: 2. Of those that a mesh axis runs over, the one named last changes fastest.
Arguments:
- hamiltonian: bfloat16 [24576, 24576], P('row', 'col'), as said below
- pattern: int32 [192, 192], P('row', 'col'), may hold values from 0 to 1, as said below
- vectors: bfloat16 [24576, 256], P('col'), may hold values from -6 to 6
Outputs:
- filtered: bfloat16 [24576, 256], P(('row', 'col'))
The draws below stay inside these ranges and needn't reach their ends.
Inputs may be any that keep to these rules, and one draw needn't show every extreme that they name: hamiltonian is exactly symmetric. pattern is symmetric, with ones on the diagonal and next to it.
All inputs are finite; a program needn't handle non-finite values.
Results may differ from the reference program's by a relative error of at most 0.018.
Values may be sent and summed in bfloat16 or wider, within the bound.
A program may use at most 32 MiB of HBM per device.

```python
import jax
import jax.numpy as jnp
from jax import lax

ORB = 128
NV = 256
NB = 192
NH = 24576


def tile_values(tile_key):
    return jax.random.normal(tile_key, (ORB, ORB), jnp.float32)


def draw_hamiltonian(key, part):
    key = jax.random.fold_in(key, 11)
    factor = 0.45 / jnp.sqrt(jnp.float32(0.5 * NB * ORB))

    def one_tile(first_idx, second_idx):
        lower = jnp.minimum(first_idx, second_idx)
        upper = jnp.maximum(first_idx, second_idx)
        values = tile_values(jax.random.fold_in(key, lower * NB + upper))
        values = jnp.where(first_idx <= second_idx, values, values.T)
        return jnp.where(first_idx == second_idx, (values + values.T) * 0.70710678, values)

    def strip_of(first_idx):
        tiles = jax.vmap(lambda second_idx: one_tile(first_idx, second_idx))(jnp.arange(NB))
        return (jnp.transpose(tiles, (1, 0, 2)).reshape(ORB, NH) * factor).astype(jnp.bfloat16)
    strips = lax.map(strip_of, jnp.arange(NB))
    return strips.reshape(NH, NH)


def draw_pattern(key, part):
    key = jax.random.fold_in(key, 12)
    coins = jax.random.randint(key, (NB, NB), 0, 2)
    rows_idx = jnp.arange(NB)[:, None]
    cols_idx = jnp.arange(NB)[None, :]
    mirrored = jnp.where(rows_idx < cols_idx, coins, coins.T)
    apart = jnp.abs(rows_idx - cols_idx)
    return jnp.where(apart <= 1, 1, mirrored).astype(jnp.int32)


def steps_of(stream_key, shape, split, least, top_value):
    level, own = 1.0, jax.random.fold_in(stream_key, 6)
    for axis_at, parts in split:
        steps = jnp.exp(jax.random.uniform(jax.random.fold_in(own, axis_at), (parts,), jnp.float32, least / len(split), top_value / len(split)))
        level = level * jnp.repeat(steps, shape[axis_at] // parts).reshape([-1 if axis == axis_at else 1 for axis in range(len(shape))])
    return level


def centred(rng, dims, width, most, cuts=(), dtype=jnp.bfloat16):
    entries = jax.random.normal(rng, dims, jnp.float32) * width
    if len(cuts) > 0:
        entries = steps_of(rng, dims, cuts, -0.22, 0.18) * entries
    return jnp.clip(entries, min=-most, max=most).astype(dtype)


def setup_inputs(seed: int = 0) -> dict:
    arg_keys = jax.random.split(jax.random.key(seed), 4)
    return {
        "hamiltonian": draw_hamiltonian(jax.random.fold_in(arg_keys[3], 71), 0),
        "pattern": draw_pattern(jax.random.fold_in(arg_keys[3], 71), 0),
        "vectors": centred(arg_keys[2], (NH, NV), 1.0, 6.0, ((0, 64),)),
    }


def reference(hamiltonian, pattern, vectors):
    blocks = hamiltonian.reshape(NB, ORB, NB, ORB)
    masked = (blocks * pattern.astype(jnp.bfloat16)[:, None, :, None]).reshape(NH, NH)
    first = jnp.dot(masked, vectors, preferred_element_type=jnp.float32).astype(jnp.bfloat16)
    second = (2.0 * jnp.dot(masked, first, preferred_element_type=jnp.float32) - vectors.astype(jnp.float32)).astype(jnp.bfloat16)
    filtered = (2.0 * jnp.dot(masked, second, preferred_element_type=jnp.float32) - first.astype(jnp.float32)).astype(jnp.bfloat16)
    return filtered
```

```python
import functools

import jax
import jax.numpy as jnp
from jax import lax
from jax.experimental import pallas as pl
from jax.experimental.pallas import tpu as pltpu
from jax.sharding import PartitionSpec as P

MESH = pl.DeviceIdType.MESH
F32, BF16 = jnp.float32, jnp.bfloat16
ORB = 128
NX, NZ, NY, NW = 4, 8, 4, 4
PIECE = 24
STACK = NZ * PIECE
HALF = NX * STACK
ROWS = 2 * HALF
COLS = 384
WIDTH = 256
CHUNKS = 2
W = WIDTH // CHUNKS
MIDDLE = 2 * PIECE
QUARTER = COLS // NY
PAIR = QUARTER // 2


def kernel(
    h_hbm, pat_ref, v_ref, out_ref,
    raw, wide, ham, ham_t, own, acc, accy, firstw,
    send_c, recv_c, send_x, recv_x, send_z, recv_z, first,
    send_y, recv_y, send_w, recv_w, second, send_f, recv_f,
    send_sem, recv_sem, load_sem,
):
    col, row = lax.axis_index("col"), lax.axis_index("row")
    core, x, z = lax.rem(col, 2), lax.rem(lax.div(col, 2), NX), lax.div(col, 2 * NX)
    y, w = lax.rem(row, NY), lax.div(row, NY)

    def device(core=core, x=x, z=z, y=y, w=w):
        return {"row": w * NY + y, "col": (z * NX + x) * 2 + core}

    def plus(at, d, n):
        return lax.rem(at + d, n)

    def minus(at, d, n):
        return lax.rem(at + n - d, n)

    def rows_at(start, size, unit):
        return pl.ds(pl.multiple_of(start, unit), size)

    other = device(core=1 - core)
    x_peer = {d: device(x=plus(x, d, NX)) for d in range(1, NX)}
    z_peer = {d: device(z=plus(z, d, NZ)) for d in range(1, NZ)}
    y_peer = {d: device(y=plus(y, d, NY)) for d in range(1, NY)}
    w_peer = [device(w=w + 1 - 2 * lax.rem(w, 2)), device(w=NW - 1 - w)]
    everyone = [other, *x_peer.values(), *z_peer.values(), *y_peer.values(), *w_peer]

    barrier = pltpu.get_barrier_semaphore()
    for peer in everyone:
        pl.semaphore_signal(barrier, inc=1, device_id=peer, device_id_type=MESH)

    used = []

    def copy(src, dst, slot, peer):
        return pltpu.make_async_remote_copy(
            src_ref=src, dst_ref=dst, send_sem=send_sem.at[slot], recv_sem=recv_sem.at[slot],
            device_id=peer, device_id_type=MESH,
        )

    def new_slot():
        used.append(None)
        return len(used) - 1

    sent = []

    def send(src, dst, slot, peer, when=None):
        def make():
            return copy(src(), dst(), slot, peer)

        sent.append((when, make))
        if when is None:
            make().start()
        else:
            pl.when(when)(lambda: make().start())

    def arrive(dst, slot, peer):
        copy(dst, dst, slot, peer).wait_recv()

    load = pltpu.make_async_copy(h_hbm, raw, load_sem)
    load.start()
    load.wait()

    @pl.loop(0, ROWS // ORB)
    def _(i):
        at = rows_at(i * ORB, ORB, ORB)
        for j in range(COLS // ORB):
            lanes = slice(j * ORB, (j + 1) * ORB)
            wide[at, lanes] = raw[at, lanes].astype(F32) * pat_ref[i, j].astype(F32)

    for k in range(2):
        for i in range(NX):
            stack = [wide[(s * 2 * NX + i * 2 + k) * PIECE:(s * 2 * NX + i * 2 + k + 1) * PIECE, :] for s in range(NZ)]
            at = (k * NX + i) * STACK
            ham[at:at + STACK, :] = jnp.concatenate(stack, axis=0).astype(BF16)

    def product_out(t, h, vec):
        theirs = rows_at((1 - core) * HALF, HALF, HALF)
        send_c[t, h] = jnp.dot(ham[theirs, :], vec, preferred_element_type=F32).astype(BF16)

    def product_own(h, vec):
        mine = rows_at(core * HALF, HALF, HALF)
        own[h] = jnp.dot(ham[mine, :], vec, preferred_element_type=F32)

    def to_core(t, h, slot):
        send(lambda: send_c.at[t, h], lambda: recv_c.at[t, h], slot, other)

    def along_x(t, slots_c):
        slots = {}
        for h in range(CHUNKS):
            arrive(recv_c.at[t, h], slots_c[h], other)
            for d in (2, 1, 3, 0):
                at = rows_at(plus(x, d, NX) * STACK, STACK, STACK)
                total = own[h, at, :] + recv_c[t, h, at, :].astype(F32)
                if d == 0:
                    acc[h] = total
                    continue
                send_x[t, h, d - 1] = total.astype(BF16)
                slots[h, d] = new_slot()
                send(functools.partial(lambda h, d: send_x.at[t, h, d - 1], h, d),
                     functools.partial(lambda h, d: recv_x.at[t, h, d - 1], h, d), slots[h, d], x_peer[d])
        return slots

    def add_x(t, h, slots):
        for d in (1, 3, 2):
            arrive(recv_x.at[t, h, d - 1], slots[h, d], x_peer[d])
        acc[h] = acc[h] + recv_x[t, h, 0].astype(F32) + recv_x[t, h, 1].astype(F32) + recv_x[t, h, 2].astype(F32)

    def vec_of(ref, h):
        return ref[:, h * W:(h + 1) * W]

    for h in range(CHUNKS):
        product_out(0, h, vec_of(v_ref, h))
        product_own(h, vec_of(v_ref, h))
    pl.semaphore_wait(barrier, len(everyone))
    slots_c = [new_slot() for _ in range(CHUNKS)]
    for h in range(CHUNKS):
        to_core(0, h, slots_c[h])
    slots_x = along_x(0, slots_c)

    for i in range(ROWS // ORB):
        ham_t[:, i * ORB:(i + 1) * ORB] = ham[i * ORB:(i + 1) * ORB, :].T

    def middle(at):
        return jnp.logical_and(at >= 2, at <= 5)

    base = (core * NX + x) * STACK
    slots_z = {}
    for h in range(CHUNKS):
        add_x(0, h, slots_x)
        send_z[h] = acc[h].astype(BF16)
        for d in (4, 5, 3, 6, 2, 7, 1):
            to = plus(z, d, NZ)
            slots_z[h, d] = new_slot()
            send(functools.partial(lambda h, to: send_z.at[h, rows_at((to - 2) * MIDDLE, MIDDLE, 16)], h, to),
                 functools.partial(lambda h, d: recv_z.at[h, d - 1], h, d), slots_z[h, d], z_peer[d], middle(to))

    slots_g = {}
    for h in range(CHUNKS):
        for d in range(1, NZ):
            slots_g[h, d] = new_slot()

        @pl.when(middle(z))
        def _(h=h):
            for d in range(1, NZ):
                arrive(recv_z.at[h, d - 1], slots_z[h, d], z_peer[d])
            total = acc[h, rows_at((z - 2) * MIDDLE, MIDDLE, 16), :]
            for d in range(1, NZ):
                total = total + recv_z[h, d - 1].astype(F32)
            first[h, rows_at(base + (z - 2) * MIDDLE, MIDDLE, 16), :] = total.astype(BF16)

        def own_middle(h=h):
            return first.at[h, rows_at(base + (z - 2) * MIDDLE, MIDDLE, 16)]

        for d in (4, 5, 3, 6, 2, 7, 1):
            send(own_middle, own_middle, slots_g[h, d], z_peer[d], middle(z))

    slots_gx, slots_gc = {}, {}

    def block(h, at_core, at_x):
        return first.at[h, rows_at((at_core * NX + at_x) * STACK, STACK, STACK)]

    for h in range(CHUNKS):
        for d in range(1, NZ):
            back = minus(z, d, NZ)

            @pl.when(middle(back))
            def _(h=h, d=d, back=back):
                arrive(first.at[h, rows_at(base + (back - 2) * MIDDLE, MIDDLE, 16)], slots_g[h, d], z_peer[d])

        mine = functools.partial(block, h, core, x)
        for d in (2, 1, 3):
            slots_gx[h, d] = new_slot()
            send(mine, mine, slots_gx[h, d], x_peer[d])
        slots_gc[h, 0] = new_slot()
        send(mine, mine, slots_gc[h, 0], other)
    for h in range(CHUNKS):
        for d in (1, 3, 2):
            back = minus(x, d, NX)
            theirs = functools.partial(block, h, core, back)
            arrive(theirs(), slots_gx[h, d], x_peer[d])
            slots_gc[h, d] = new_slot()
            send(theirs, theirs, slots_gc[h, d], other)

    slots_y = {}
    for h in range(CHUNKS):
        for d in range(NX):
            arrive(block(h, 1 - core, minus(x, d, NX)), slots_gc[h, d], other)
        own[h, 0:COLS, :] = jnp.dot(ham_t[...], first[h], preferred_element_type=F32)
        for d in (2, 1, 3):
            send_y[h, d - 1] = own[h, rows_at(plus(y, d, NY) * QUARTER, QUARTER, 16), :].astype(BF16)
            slots_y[h, d] = new_slot()
            send(functools.partial(lambda h, d: send_y.at[h, d - 1], h, d),
                 functools.partial(lambda h, d: recv_y.at[h, d - 1], h, d), slots_y[h, d], y_peer[d])
        accy[h] = own[h, rows_at(y * QUARTER, QUARTER, 16), :]

    def exchange_w(stage, h, slots):
        for g in range(2):
            send_w[stage, h, g] = accy[h, g * PAIR:(g + 1) * PAIR, :].astype(BF16)
            slots[stage, h, g] = new_slot()
            send(functools.partial(lambda g: send_w.at[stage, h, g], g),
                 functools.partial(lambda g: recv_w.at[stage, h, g], g), slots[stage, h, g], w_peer[(g + stage) % 2])

    def add_w(stage, h, slots):
        for g in range(2):
            arrive(recv_w.at[stage, h, g], slots[stage, h, g], w_peer[(g + stage) % 2])
            accy[h, g * PAIR:(g + 1) * PAIR, :] = accy[h, g * PAIR:(g + 1) * PAIR, :] + recv_w[stage, h, g].astype(F32)

    slots_w = {}
    for h in range(CHUNKS):
        for d in (1, 3, 2):
            arrive(recv_y.at[h, d - 1], slots_y[h, d], y_peer[d])
        accy[h] = accy[h] + recv_y[h, 0].astype(F32) + recv_y[h, 1].astype(F32) + recv_y[h, 2].astype(F32)
        exchange_w(0, h, slots_w)
    for h in range(CHUNKS):
        add_w(0, h, slots_w)
        exchange_w(1, h, slots_w)
    slots_s = {}
    quarter = rows_at(y * QUARTER, QUARTER, 16)
    for h in range(CHUNKS):
        add_w(1, h, slots_w)
        before = v_ref[quarter, h * W:(h + 1) * W].astype(F32)
        second[h, quarter, :] = (2.0 * accy[h] - before).astype(BF16)
        for d in (2, 1, 3):
            slots_s[h, d] = new_slot()
            place = functools.partial(lambda h: second.at[h, quarter], h)
            send(place, place, slots_s[h, d], y_peer[d])

    slots_c = []
    for h in range(CHUNKS):
        for d in (1, 3, 2):
            arrive(second.at[h, rows_at(minus(y, d, NY) * QUARTER, QUARTER, 16)], slots_s[h, d], y_peer[d])
        product_out(1, h, second[h])
        slots_c.append(new_slot())
        to_core(1, h, slots_c[h])
        product_own(h, second[h])
    slots_x = along_x(1, slots_c)
    for h in range(CHUNKS):
        firstw[h] = first[h, rows_at(base, STACK, STACK), :].astype(F32)

    def folded(ref, at):
        rows = rows_at(at * PIECE, PIECE, 8)
        halves = [ref[0, rows, :], ref[1, rows, :]] if CHUNKS == 2 else [ref[0, rows, :ORB], ref[0, rows, ORB:]]
        return jnp.concatenate(halves, axis=0)

    for h in range(CHUNKS):
        add_x(1, h, slots_x)
    slots_f = {}
    for d in (4, 5, 3, 6, 2, 7, 1):
        send_f[d - 1] = folded(acc, plus(z, d, NZ)).astype(BF16)
        slots_f[d] = new_slot()
        send(functools.partial(lambda d: send_f.at[d - 1], d), functools.partial(lambda d: recv_f.at[d - 1], d),
             slots_f[d], z_peer[d])
    total = folded(acc, z)
    for d in (1, 7, 2, 6, 3, 5, 4):
        arrive(recv_f.at[d - 1], slots_f[d], z_peer[d])
        total = total + recv_f[d - 1].astype(F32)
    result = 2.0 * total - folded(firstw, z)
    out_ref[:, :ORB] = result[:PIECE].astype(BF16)
    out_ref[:, ORB:] = result[PIECE:].astype(BF16)

    for when, make in sent:
        if when is None:
            make().wait_send()
        else:
            pl.when(when)(lambda make=make: make().wait_send())


def slots_needed():
    per_chunk = 2 * (1 + 3) + 2 * 7 + 3 + 4 + 3 + 4 + 3
    return CHUNKS * per_chunk + 7


def body(hamiltonian, pattern, vectors):
    vm = pltpu.VMEM
    n = CHUNKS
    scratch = [
        vm((ROWS, COLS), BF16), vm((ROWS, COLS), F32), vm((ROWS, COLS), BF16), vm((COLS, ROWS), BF16),
        vm((n, HALF, W), F32), vm((n, STACK, W), F32), vm((n, QUARTER, W), F32), vm((n, STACK, W), F32),
        vm((2, n, HALF, W), BF16), vm((2, n, HALF, W), BF16),
        vm((2, n, 3, STACK, W), BF16), vm((2, n, 3, STACK, W), BF16),
        vm((n, STACK, W), BF16), vm((n, 7, MIDDLE, W), BF16), vm((n, ROWS, W), BF16),
        vm((n, 3, QUARTER, W), BF16), vm((n, 3, QUARTER, W), BF16),
        vm((2, n, 2, PAIR, W), BF16), vm((2, n, 2, PAIR, W), BF16), vm((n, COLS, W), BF16),
        vm((7, 2 * PIECE, ORB), BF16), vm((7, 2 * PIECE, ORB), BF16),
        pltpu.SemaphoreType.DMA((slots_needed(),)), pltpu.SemaphoreType.DMA((slots_needed(),)),
        pltpu.SemaphoreType.DMA,
    ]
    return pl.pallas_call(
        kernel,
        out_shape=jax.ShapeDtypeStruct((PIECE, WIDTH), BF16),
        in_specs=[
            pl.BlockSpec(memory_space=pl.ANY),
            pl.BlockSpec(memory_space=pltpu.SMEM),
            pl.BlockSpec(memory_space=pltpu.VMEM),
        ],
        out_specs=pl.BlockSpec(memory_space=pltpu.VMEM),
        scratch_shapes=scratch,
        compiler_params=pltpu.CompilerParams(collective_id=0, has_side_effects=True, vmem_limit_bytes=40 * 2**20),
        cost_estimate=pl.CostEstimate(flops=6 * ROWS * COLS * WIDTH, bytes_accessed=2 * ROWS * COLS, transcendentals=0),
        name="filter_kernel",
    )(hamiltonian, pattern, vectors)


def solution(mesh):
    in_specs = (P("row", "col"), P("row", "col"), P("col", None))
    out_specs = P(("row", "col"), None)
    return jax.shard_map(body, mesh=mesh, in_specs=in_specs, out_specs=out_specs, check_vma=False)
```

```python
import jax
import jax.numpy as jnp
from jax import lax
from jax.experimental import pallas as pl
from jax.experimental.pallas import tpu as pltpu
from jax.sharding import PartitionSpec as P

MESH = pl.DeviceIdType.MESH
F32, BF16 = jnp.float32, jnp.bfloat16
ORB = 128
NX, NZ, NY, NW = 4, 8, 4, 4
NQ = 4
BLOCK = 384
PIECE = 24
PART = 2 * PIECE
CHUNK = NX * PART
HALF = NQ * CHUNK
ROWS = 2 * HALF
COLS = 384
WIDTH = 256
QUARTER = COLS // NY
PAIR = QUARTER // 2

C_AT = 0
X_AT = C_AT + 2 * NQ
Z_AT = X_AT + 2 * NQ * 3
G_AT = Z_AT + 7
GX_AT = G_AT + 7
GC_AT = GX_AT + NQ * 3
Y_AT = GC_AT + NQ
W_AT = Y_AT + 6
S_AT = W_AT + 8
F_AT = S_AT + 6
SLOTS = F_AT + 8


def kernel(
    h_hbm, pat_hbm, v_hbm, out_ref,
    raw, pat_ref, v_ref, wide, ham, ham_t, flat, own, acc, prod, accy, firstw, lastw,
    send_c, recv_c, send_x, recv_x, send_z, recv_z, first,
    send_y, recv_y, send_w, recv_w, second, send_f, recv_f,
    send_sem, recv_sem, load_sem,
):
    col, row = lax.axis_index("col"), lax.axis_index("row")
    core, x, z = lax.rem(col, 2), lax.rem(lax.div(col, 2), NX), lax.div(col, 2 * NX)
    y, w = lax.rem(row, NY), lax.div(row, NY)

    def device(core=core, x=x, z=z, y=y, w=w):
        return {"row": w * NY + y, "col": (z * NX + x) * 2 + core}

    def plus(at, d, n):
        return lax.rem(at + d, n)

    def minus(at, d, n):
        return lax.rem(at + n - d, n)

    def rows_at(start, size, unit):
        return pl.ds(pl.multiple_of(start, unit), size)

    other = device(core=1 - core)
    x_peer = {d: device(x=plus(x, d, NX)) for d in range(1, NX)}
    z_peer = {d: device(z=plus(z, d, NZ)) for d in range(1, NZ)}
    y_peer = {d: device(y=plus(y, d, NY)) for d in range(1, NY)}
    w_peer = [device(w=w + 1 - 2 * lax.rem(w, 2)), device(w=NW - 1 - w)]

    greeted = [other, *x_peer.values(), *y_peer.values(), *z_peer.values(), *w_peer]
    barrier = pltpu.get_barrier_semaphore()
    for peer in greeted:
        pl.semaphore_signal(barrier, inc=1, device_id=peer, device_id_type=MESH)

    sent = []

    def send(src, dst, slot, peer, when=None, recv_slot=None):
        def make():
            return pltpu.make_async_remote_copy(
                src_ref=src(), dst_ref=dst(), send_sem=send_sem.at[slot],
                recv_sem=recv_sem.at[slot if recv_slot is None else recv_slot], device_id=peer, device_id_type=MESH,
            )

        sent.append((when, make))
        if when is None:
            make().start()
        else:
            pl.when(when)(lambda: make().start())

    def all_left():
        for when, make in sent:
            if when is None:
                make().wait_send()
            else:
                pl.when(when)(lambda make=make: make().wait_send())
        sent.clear()

    def arrive(dst, slot, peer):
        pltpu.make_async_remote_copy(
            src_ref=dst, dst_ref=dst, send_sem=send_sem.at[0], recv_sem=recv_sem.at[slot],
            device_id=peer, device_id_type=MESH,
        ).wait_recv()

    low = 1 - lax.div(z, NZ // 2)

    def place_of(q):
        return low * (NQ - 1 - q) + (1 - low) * q

    far_q = [place_of(k) for k in range(NQ)]

    def chunk_rows(at_core, q):
        return rows_at((at_core * NQ + q) * CHUNK, CHUNK, CHUNK)

    def part_rows(q, at_x):
        return rows_at(((core * NQ + q) * NX + at_x) * PART, PART, PART)

    def load(k):
        at = rows_at(place_of(k) * BLOCK, BLOCK, BLOCK)
        return pltpu.make_async_copy(h_hbm.at[at], raw.at[at], load_sem.at[k])

    pat_load = pltpu.make_async_copy(pat_hbm, pat_ref, load_sem.at[NQ])
    v_load = pltpu.make_async_copy(v_hbm, v_ref, load_sem.at[NQ + 1])
    pat_load.start()
    v_load.start()
    for k in range(NQ):
        load(k).start()

    def mask(k):
        for i in range(BLOCK // ORB):
            tile = place_of(k) * (BLOCK // ORB) + i
            at = rows_at(tile * ORB, ORB, ORB)
            for j in range(COLS // ORB):
                lanes = slice(j * ORB, (j + 1) * ORB)
                raw[at, lanes] = (raw[at, lanes].astype(F32) * pat_ref[j, tile].astype(F32)).astype(BF16)

    def reorder():
        @pl.loop(0, ROWS // ORB)
        def _(i):
            at = rows_at(i * ORB, ORB, ORB)
            wide[at, :] = raw[at, :].astype(F32)

        @pl.loop(0, 2 * NQ)
        def _(n):
            k, q = lax.div(n, NQ), lax.rem(n, NQ)
            stack = []
            for i in range(NX):
                for j in range(2):
                    at = ((2 * q + j) * 2 * NX + i * 2 + k) * PIECE
                    stack.append(wide[rows_at(at, PIECE, 8), :])
            ham[rows_at(n * CHUNK, CHUNK, CHUNK), :] = jnp.concatenate(stack, axis=0).astype(BF16)

    def transpose():
        @pl.loop(0, ROWS // ORB)
        def _(n):
            k, i = lax.div(n, HALF // ORB), lax.rem(n, HALF // ORB)
            ham_t[k, :, rows_at(i * ORB, ORB, ORB)] = ham[rows_at(n * ORB, ORB, ORB), :].T

    def share(k, at_core):
        stack = []
        for i in range(NX):
            for j in range(2):
                stack.append(flat[k, rows_at((j * 2 * NX + i * 2 + at_core) * PIECE, PIECE, 8), :])
        return jnp.concatenate(stack, axis=0)

    def product_out(t, k, vec):
        send_c[t, k] = jnp.dot(ham[chunk_rows(1 - core, far_q[k]), :], vec, preferred_element_type=F32).astype(BF16)

    def product_own(k, vec):
        own[k] = jnp.dot(ham[chunk_rows(core, far_q[k]), :], vec, preferred_element_type=F32)

    def to_core(t, k):
        send(lambda: send_c.at[t, k], lambda: recv_c.at[t, k], C_AT + t * NQ + k, other)

    def along_x(t, k):
        arrive(recv_c.at[t, k], C_AT + t * NQ + k, other)
        for d in (2, 1, 3, 0):
            at = rows_at(plus(x, d, NX) * PART, PART, PART)
            total = own[k, at, :] + recv_c[t, k, at, :].astype(F32)
            if d == 0:
                acc[k] = total
                continue
            send_x[t, k, d - 1] = total.astype(BF16)
            send(lambda d=d: send_x.at[t, k, d - 1], lambda d=d: recv_x.at[t, k, d - 1],
                 X_AT + (t * NQ + k) * 3 + d - 1, x_peer[d])

    def add_x(t, k):
        for d in (1, 3, 2):
            arrive(recv_x.at[t, k, d - 1], X_AT + (t * NQ + k) * 3 + d - 1, x_peer[d])
        total = acc[k]
        for d in range(3):
            total = total + recv_x[t, k, d].astype(F32)
        acc[k] = total

    pat_load.wait()
    v_load.wait()
    vec = v_ref[...]

    @pl.loop(0, NQ)
    def _(k):
        load(k).wait()
        mask(k)
        flat[k] = jnp.dot(raw[rows_at(place_of(k) * BLOCK, BLOCK, BLOCK), :], vec, preferred_element_type=F32)
        send_c[0, k] = share(k, 1 - core).astype(BF16)

    pl.semaphore_wait(barrier, len(greeted))
    for k in range(NQ):
        to_core(0, k)

    @pl.loop(0, NQ)
    def _(k):
        own[k] = share(k, core)

    for k in range(NQ):
        along_x(0, k)
    reorder()

    def apart(to):
        return lax.rem(to - z + NZ, NZ) - 1

    in_middle = jnp.logical_and(z >= 2, z <= 5)
    for k in range(NQ):
        add_x(0, k)
        send_z[k] = acc[k].astype(BF16)
        to = far_q[k] + 2
        send(lambda k=k: send_z.at[k], lambda to=to: recv_z.at[apart(to)], Z_AT + k, device(z=to), to != z,
             Z_AT + apart(to))

    transpose()

    @pl.when(in_middle)
    def _():
        total = acc[place_of(z - 2)]
        for d in (1, 7, 2, 6, 3, 5, 4):
            arrive(recv_z.at[d - 1], Z_AT + d - 1, z_peer[d])
            total = total + recv_z[d - 1].astype(F32)
        first[part_rows(z - 2, x), :] = total.astype(BF16)

    for d in (4, 5, 3, 6, 2, 7, 1):
        send(lambda: first.at[part_rows(z - 2, x)], lambda: first.at[part_rows(z - 2, x)], G_AT + d - 1, z_peer[d],
             in_middle)

    for k in range(NQ):
        q = far_q[NQ - 1 - k]
        source = q + 2
        mine = part_rows(q, x)

        @pl.when(source != z)
        def _(source=source, mine=mine):
            arrive(first.at[mine], G_AT + lax.rem(z - source + NZ, NZ) - 1, device(z=source))

        for d in (2, 1, 3):
            send(lambda mine=mine: first.at[mine], lambda mine=mine: first.at[mine], GX_AT + k * 3 + d - 1, x_peer[d])
    for k in range(NQ):
        q = far_q[NQ - 1 - k]
        for d in (1, 3, 2):
            arrive(first.at[part_rows(q, minus(x, d, NX))], GX_AT + k * 3 + d - 1, x_peer[d])
        send(lambda q=q: first.at[chunk_rows(core, q)], lambda q=q: first.at[chunk_rows(core, q)], GC_AT + k, other)

    def half_rows(at_core):
        return rows_at(at_core * HALF, HALF, HALF)

    prod[...] = jnp.dot(ham_t[core], first[half_rows(core), :], preferred_element_type=F32)
    for k in range(NQ):
        arrive(first.at[chunk_rows(1 - core, far_q[NQ - 1 - k])], GC_AT + k, other)
    prod[...] += jnp.dot(ham_t[1 - core], first[half_rows(1 - core), :], preferred_element_type=F32)
    for h in range(2):
        lanes = slice(h * ORB, (h + 1) * ORB)
        for d in (2, 1, 3):
            send_y[h, d - 1] = prod[rows_at(plus(y, d, NY) * QUARTER, QUARTER, 16), lanes].astype(BF16)
            send(lambda h=h, d=d: send_y.at[h, d - 1], lambda h=h, d=d: recv_y.at[h, d - 1], Y_AT + h * 3 + d - 1,
                 y_peer[d])

    def w_slot(stage, h, g):
        return W_AT + (stage * 2 + h) * 2 + g

    def exchange_w(stage, h, g):
        send_w[stage, h, g] = accy[h, g * PAIR:(g + 1) * PAIR, :].astype(BF16)
        send(lambda: send_w.at[stage, h, g], lambda: recv_w.at[stage, h, g], w_slot(stage, h, g),
             w_peer[(g + stage) % 2])

    def add_w(stage, h, g):
        arrive(recv_w.at[stage, h, g], w_slot(stage, h, g), w_peer[(g + stage) % 2])
        accy[h, g * PAIR:(g + 1) * PAIR, :] += recv_w[stage, h, g].astype(F32)

    quarter = rows_at(y * QUARTER, QUARTER, 16)
    for h in range(2):
        for d in (1, 3, 2):
            arrive(recv_y.at[h, d - 1], Y_AT + h * 3 + d - 1, y_peer[d])
        total = prod[quarter, h * ORB:(h + 1) * ORB]
        for d in range(3):
            total = total + recv_y[h, d].astype(F32)
        accy[h] = total
        exchange_w(0, h, 0)
        exchange_w(0, h, 1)
    all_left()
    for h in range(2):
        for g in range(2):
            add_w(0, h, g)
            exchange_w(1, h, g)
    for h in range(2):
        lanes = slice(h * ORB, (h + 1) * ORB)
        add_w(1, h, 0)
        add_w(1, h, 1)
        second[quarter, lanes] = (2.0 * accy[h] - v_ref[quarter, lanes].astype(F32)).astype(BF16)
        for d in (2, 1, 3):
            send(lambda h=h: second.at[quarter, pl.ds(h * ORB, ORB)],
                 lambda h=h: second.at[quarter, pl.ds(h * ORB, ORB)], S_AT + h * 3 + d - 1, y_peer[d])

    for h in range(2):
        for d in (1, 3, 2):
            arrive(second.at[rows_at(minus(y, d, NY) * QUARTER, QUARTER, 16), pl.ds(h * ORB, ORB)],
                   S_AT + h * 3 + d - 1, y_peer[d])
    vec = second[...]
    for k in range(NQ):
        product_out(1, k, vec)
        to_core(1, k)
    for k in range(NQ):
        product_own(k, vec)
        along_x(1, k)
    firstw[...] = first[part_rows(lax.div(z, 2), x), :].astype(F32)

    def folded(value):
        return jnp.concatenate([value[:, :ORB], value[:, ORB:]], axis=0)

    for k in range(NQ):
        add_x(1, k)
        for j in range(2):
            n = k * 2 + j
            to = far_q[k] * 2 + j
            send_f[n] = folded(acc[k, j * PIECE:(j + 1) * PIECE, :]).astype(BF16)
            send(lambda n=n: send_f.at[n], lambda to=to: recv_f.at[apart(to)], F_AT + n, device(z=to), to != z,
                 F_AT + apart(to))
    all_left()
    odd = rows_at(lax.rem(z, 2) * PIECE, PIECE, 8)
    lastw[...] = acc[place_of(lax.div(z, 2))]
    total = folded(lastw[odd, :])
    before = folded(firstw[odd, :])
    for d in (1, 7, 2, 6, 3, 5, 4):
        arrive(recv_f.at[d - 1], F_AT + d - 1, z_peer[d])
        total = total + recv_f[d - 1].astype(F32)
    result = 2.0 * total - before
    out_ref[:, :ORB] = result[:PIECE].astype(BF16)
    out_ref[:, ORB:] = result[PIECE:].astype(BF16)


def body(hamiltonian, pattern, vectors):
    vm = pltpu.VMEM
    scratch = [
        vm((ROWS, COLS), BF16), pltpu.SMEM((COLS // ORB, ROWS // ORB), jnp.int32), vm((COLS, WIDTH), BF16),
        vm((ROWS, COLS), F32), vm((ROWS, COLS), BF16), vm((2, COLS, HALF), BF16),
        vm((NQ, BLOCK, WIDTH), F32), vm((NQ, CHUNK, WIDTH), F32), vm((NQ, PART, WIDTH), F32), vm((COLS, WIDTH), F32), vm((2, QUARTER, ORB), F32),
        vm((PART, WIDTH), F32), vm((PART, WIDTH), F32),
        vm((2, NQ, CHUNK, WIDTH), BF16), vm((2, NQ, CHUNK, WIDTH), BF16),
        vm((2, NQ, 3, PART, WIDTH), BF16), vm((2, NQ, 3, PART, WIDTH), BF16),
        vm((NQ, PART, WIDTH), BF16), vm((7, PART, WIDTH), BF16), vm((ROWS, WIDTH), BF16),
        vm((2, 3, QUARTER, ORB), BF16), vm((2, 3, QUARTER, ORB), BF16),
        vm((2, 2, 2, PAIR, ORB), BF16), vm((2, 2, 2, PAIR, ORB), BF16), vm((COLS, WIDTH), BF16),
        vm((8, PART, ORB), BF16), vm((7, PART, ORB), BF16),
        pltpu.SemaphoreType.DMA((SLOTS,)), pltpu.SemaphoreType.DMA((SLOTS,)), pltpu.SemaphoreType.DMA((NQ + 2,)),
    ]
    return pl.pallas_call(
        kernel,
        out_shape=jax.ShapeDtypeStruct((PIECE, WIDTH), BF16),
        in_specs=[pl.BlockSpec(memory_space=pl.ANY)] * 3,
        out_specs=pl.BlockSpec(memory_space=pltpu.VMEM),
        scratch_shapes=scratch,
        compiler_params=pltpu.CompilerParams(collective_id=0, has_side_effects=True, vmem_limit_bytes=60 * 2**20),
        cost_estimate=pl.CostEstimate(flops=6 * ROWS * COLS * WIDTH, bytes_accessed=2 * ROWS * COLS, transcendentals=0),
        name="filter_kernel",
    )(hamiltonian, pattern.T, vectors)


def solution(mesh):
    in_specs = (P("row", "col"), P("row", "col"), P("col", None))
    out_specs = P(("row", "col"), None)
    return jax.shard_map(body, mesh=mesh, in_specs=in_specs, out_specs=out_specs, check_vma=False)
```
